512 devices in a mesh: dp: 16 (over z), seq: 32 (over x, y, core).
Axes of the slice: x: 4, y: 4, z: 16, core: 2. Of those that a mesh axis runs over, the one named last changes fastest.
Arguments:
- latents: bfloat16 [16, 4096, 3072], P('dp', 'seq'), may hold values from -6 to 6
- modulation_shift: bfloat16 [16, 3, 3072], P('dp'), may hold values from -3 to 3
- modulation_scale: bfloat16 [16, 3, 3072], P('dp'), may hold values from -1.5 to 1.5
- query: bfloat16 [16, 4096, 3072], P('dp', 'seq'), may hold values from -6 to 6
- key: bfloat16 [16, 4096, 3072], P('dp', 'seq'), may hold values from -6 to 6
- value: bfloat16 [16, 4096, 3072], P('dp', 'seq'), may hold values from -6 to 6
- adapter_down_weight: bfloat16 [3072, 128], replicated, may hold values from -0.109375 to 0.109375
- adapter_up_weight: bfloat16 [128, 3072], replicated, may hold values from -1.5 to 1.5
- adapter_index: int32 [16, 4096, 2], P('dp', 'seq'), may hold values from 0 to 7, all different within a row
- adapter_weight: float32 [16, 4096, 2], P('dp', 'seq'), may hold values from 0.3 to 1.2
- sequence_length: int32 [16, 3], P('dp'), may hold values from 1 to 3072, 4096 in all within a row
Outputs:
- attended: bfloat16 [16, 4096, 3072], P('dp', 'seq')
The draws below stay inside these ranges and needn't reach their ends.
Inputs may be any that keep to these rules, and one draw needn't show every extreme that they name: `sequence_length`: each pack's lengths sum to 4096 and its longest sequence has exactly 3072 tokens. `adapter_index`: the 2 LoRAs of a token are different.
All inputs are finite; a program needn't handle non-finite values.
Results may differ from the reference program's by a relative error of at most 0.0058.
Values may be sent and summed in bfloat16 or wider, within the bound.
No kernel may reach another device: no remote copies, remote signals or barrier semaphores. Data moves between devices by JAX's collectives and lax.ppermute only.
A program may use at most 128 MiB of HBM per device.

```python
import math
import jax
import jax.numpy as jnp
import numpy as np
from jax import lax

HEADS = 24
HEAD_DIM = 128
MODEL_WIDTH = 3072
STYLE_ADAPTERS = 8
ADAPTER_RANK = 16
TOKEN_ADAPTERS = 2
NSEG = 3
PACK_TOKENS = 4096
PACK_COUNT = 16
MOST = 3072


def draw_query(key, part):
    key = jax.random.fold_in(key, 1)
    result = jnp.clip(1.5 * jax.random.normal(key, (PACK_COUNT, PACK_TOKENS, MODEL_WIDTH), jnp.float32), -6.0, 6.0)
    return result.astype(jnp.bfloat16)


def draw_key(key, part):
    key = jax.random.fold_in(key, 2)
    result = jnp.clip(1.5 * jax.random.normal(key, (PACK_COUNT, PACK_TOKENS, MODEL_WIDTH), jnp.float32), -6.0, 6.0)
    return result.astype(jnp.bfloat16)


def block_levels(key, dims, pieces, low, high):
    level = 1.0
    for position, blocks in pieces:
        heights = jax.random.uniform(jax.random.fold_in(jax.random.fold_in(key, 6), position), (blocks,), jnp.float32, low / len(pieces), high / len(pieces))
        level = level * jnp.repeat(jnp.exp(heights), dims[position] // blocks).reshape((-1,) + (1,) * (len(dims) - 1 - position))
    return level


def distinct(rng, rows, number_of, top, lift):
    sequence = jax.random.permutation(jax.random.fold_in(rng, 1), number_of)
    pull = sequence
    for power in range(3):
        pull = pull * pull // number_of
    pull = pull * lift // number_of
    lots = jax.random.randint(jax.random.fold_in(rng, 2), (rows, number_of), 0, 4096) + pull
    fixed_rows = jax.random.permutation(jax.random.fold_in(rng, 3), rows)[jnp.arange(number_of) % rows]
    lots = jnp.where(jnp.arange(rows)[:, None] == fixed_rows[None, :], 1 << 14, lots)
    score = lots * number_of + jnp.arange(number_of)
    return lax.top_k(score.astype(jnp.int32), top)[1].astype(jnp.int32)


def length_profile(count, total, bound, skew):
    loads = [(1 << 20) // math.isqrt(grade ** skew) + 1 for grade in range(2, count + 1)]
    surplus, holding = total - bound - (count - 1), [1] * (count - 1)
    while surplus > 0:
        candidates = [i for i in range(count - 1) if holding[i] < bound]
        pool, budget = sum([loads[i] for i in candidates]), surplus
        for i in candidates:
            more = min(bound - holding[i], max(1, budget * loads[i] // pool), surplus)
            holding[i] = holding[i] + more
            surplus = surplus - more
    return np.array([bound] + holding)


def ragged(key, count, total, most, skew):
    if count == 2:
        one = jax.random.randint(key, (), max(1, total - most), min(most, total - 1) + 1)
        return jnp.stack([one, total - one])
    sizes = jnp.asarray(length_profile(count, total, most, skew), jnp.int32)
    couples = (count - 1) // 2
    giver, sink = sizes[1:1 + 2 * couples:2], sizes[2:2 + 2 * couples:2]
    room = jnp.minimum(giver - 1, most - sink)
    passed = jax.random.randint(jax.random.fold_in(key, 1), (couples,), 0, 1 << 20) % (room + 1)
    sizes = sizes.at[1:1 + 2 * couples:2].set(giver - passed).at[2:2 + 2 * couples:2].set(sink + passed)
    return sizes[jax.random.permutation(jax.random.fold_in(key, 2), count)]


def centred(key, extent, spread, most, shards=(), kind=jnp.bfloat16):
    values = jax.random.normal(key, extent, jnp.float32) * spread
    if len(shards) > 0:
        values = block_levels(key, extent, shards, -0.22, 0.18) * values
    return jnp.clip(values, min=-most, max=most).astype(kind)


def setup_inputs(seed: int = 0) -> dict:
    splits = jax.random.split(jax.random.key(seed), 12)
    return {
        "latents": centred(splits[0], (PACK_COUNT, PACK_TOKENS, MODEL_WIDTH), 1.0, 6.0, ((0, 16), (1, 32))),
        "modulation_shift": centred(splits[1], (PACK_COUNT, NSEG, MODEL_WIDTH), 0.5, 3.0, ((0, 16),)),
        "modulation_scale": centred(splits[2], (PACK_COUNT, NSEG, MODEL_WIDTH), 0.3, 1.5, ((0, 16),)),
        "query": draw_query(jax.random.fold_in(splits[11], 71), 0),
        "key": draw_key(jax.random.fold_in(splits[11], 71), 0),
        "value": centred(splits[5], (PACK_COUNT, PACK_TOKENS, MODEL_WIDTH), 1.0, 6.0, ((0, 16), (1, 32))),
        "adapter_down_weight": centred(splits[6], (MODEL_WIDTH, STYLE_ADAPTERS * ADAPTER_RANK), MODEL_WIDTH ** -0.5, 0.109375),
        "adapter_up_weight": centred(splits[7], (STYLE_ADAPTERS * ADAPTER_RANK, MODEL_WIDTH), ADAPTER_RANK ** -0.5, 1.5),
        "adapter_index": distinct(splits[8], PACK_COUNT * PACK_TOKENS, STYLE_ADAPTERS, TOKEN_ADAPTERS, 2048).reshape((PACK_COUNT, PACK_TOKENS, TOKEN_ADAPTERS)),
        "adapter_weight": jnp.clip(0.3 + 0.90000004 * jax.random.uniform(splits[9], (PACK_COUNT, PACK_TOKENS, TOKEN_ADAPTERS), jnp.float32) ** block_levels(splits[9], (PACK_COUNT, PACK_TOKENS, TOKEN_ADAPTERS), ((0, 16), (1, 32)), -0.2, 0.2), 0.3, 1.2),
        "sequence_length": jax.vmap(lambda own: ragged(own, NSEG, PACK_TOKENS, MOST, 1))(jax.random.split(splits[10], PACK_COUNT)).reshape((PACK_COUNT, NSEG)).astype(jnp.int32),
    }


mask_value = -1e+30
epsilon = 1e-06

def segment_ids(lengths, count):
    bounds = jnp.cumsum(lengths)[:-1]
    positions = jnp.arange(count, dtype=jnp.int32)
    return lax.optimization_barrier(jnp.sum((positions[:, None] >= bounds[None, :]).astype(jnp.int32), axis=1)).astype(jnp.int32)

def reference(latents, modulation_shift, modulation_scale, query, key, value, adapter_down_weight, adapter_up_weight, adapter_index, adapter_weight, sequence_length):

    def single_pack(items):
        latent, shift, scales, queries, keys, value_rows, adapter_picks, mixes, lengths = items
        segment = segment_ids(lengths, PACK_TOKENS)
        onehot = (segment[:, None] == jnp.arange(NSEG, dtype=jnp.int32)[None, :]).astype(jnp.bfloat16)
        shift_rows = jnp.dot(onehot, shift, preferred_element_type=jnp.float32)
        scale_rows = jnp.dot(onehot, scales, preferred_element_type=jnp.float32)
        floats = latent.astype(jnp.float32)
        center = lax.optimization_barrier(jnp.mean(floats, axis=1, keepdims=True))
        variance = lax.optimization_barrier(jnp.mean(jnp.square(floats - center), axis=1, keepdims=True))
        normed = (floats - center) / jnp.sqrt(variance + epsilon)
        modulated_input = ((1.0 + scale_rows) * normed + shift_rows).astype(jnp.bfloat16)
        reduced_value = jnp.dot(modulated_input, adapter_down_weight, preferred_element_type=jnp.float32)
        selected_adapter = (adapter_picks[:, :, None] == jnp.arange(STYLE_ADAPTERS, dtype=jnp.int32)[None, None, :]).astype(jnp.float32)
        mixing_weight = lax.optimization_barrier(jnp.sum(mixes[:, :, None] * selected_adapter, axis=1))
        weighted_update = (reduced_value * jnp.repeat(mixing_weight, ADAPTER_RANK, axis=1)).astype(jnp.bfloat16)
        blended_values = (value_rows.astype(jnp.float32) + jnp.dot(weighted_update, adapter_up_weight, preferred_element_type=jnp.float32)).astype(jnp.bfloat16)
        same = segment[:, None] == segment[None, :]
        q_heads = queries.reshape(PACK_TOKENS, HEADS, HEAD_DIM).transpose(1, 0, 2)
        k_heads = keys.reshape(PACK_TOKENS, HEADS, HEAD_DIM).transpose(1, 0, 2)
        v_heads = blended_values.reshape(PACK_TOKENS, HEADS, HEAD_DIM).transpose(1, 0, 2)
        factor = 1.0 / math.sqrt(HEAD_DIM)

        def one_head(parts):
            q_head, k_head, v_head = parts
            scores = jnp.dot(q_head, k_head.T, preferred_element_type=jnp.float32) * factor
            scores = jnp.where(same, scores, mask_value)
            largest = lax.optimization_barrier(jnp.max(scores, axis=1, keepdims=True))
            expo = jnp.exp(scores - largest)
            totals = lax.optimization_barrier(jnp.sum(expo, axis=1, keepdims=True))
            return jnp.dot(expo.astype(jnp.bfloat16), v_head, preferred_element_type=jnp.float32) / totals
        heads_out = lax.map(one_head, (q_heads, k_heads, v_heads))
        return heads_out.transpose(1, 0, 2).reshape(PACK_TOKENS, HEADS * HEAD_DIM).astype(jnp.bfloat16)
    return lax.map(single_pack, (latents, modulation_shift, modulation_scale, query, key, value, adapter_index, adapter_weight, sequence_length))
```

```python
import functools
import math

import jax
import jax.numpy as jnp
from jax import lax
from jax.experimental import pallas as pl
from jax.experimental.pallas import tpu as pltpu
from jax.sharding import PartitionSpec as P

HEADS = 24
HEAD_DIM = 128
STYLE_ADAPTERS = 8
ADAPTER_RANK = 16
ROWS = 128
CHIPS = 16
PACK_TOKENS = 4096
BLOCKS = PACK_TOKENS // ROWS
HALF = ROWS // 2
Q_ROWS = ROWS + HALF
K_AT = Q_ROWS
V_AT = K_AT + 2 * ROWS
PIECE = V_AT + 2 * ROWS
KV_ROWS = 4 * ROWS
STEP = 8
TILE = 512

mask_value = -1e30
epsilon = 1e-06
to_base2 = math.log2(math.e) / math.sqrt(HEAD_DIM)


def heads_of(chip):
    trio = 3 * (chip // 2)
    if chip % 2 == 0:
        return trio, trio + 1, 0
    return trio + 2, trio + 1, HALF


def columns(head):
    return slice(head * HEAD_DIM, (head + 1) * HEAD_DIM)


def prepare_kernel(
    lengths, latents, shift, scale, query, key, value, down, up, index, weight, send,
    latents_in, query_in, key_in, value_in, down_in, up_in, stage, in_sems, out_sems,
):
    pairs = (
        (latents, latents_in),
        (down, down_in),
        (query, query_in),
        (key, key_in),
        (up, up_in),
        (value, value_in),
    )
    loads = [
        pltpu.make_async_copy(source, target, in_sems.at[n])
        for n, (source, target) in enumerate(pairs)
    ]
    for load in loads:
        load.start()
    first = lengths[0, 0]
    second = first + lengths[0, 1]
    start = lax.axis_index("seq") * ROWS
    positions = start + lax.broadcasted_iota(jnp.int32, (ROWS, 1), 0)
    adapter = lax.broadcasted_iota(jnp.int32, (ROWS, ROWS), 0) // ADAPTER_RANK
    coefficient = jnp.zeros((ROWS, ROWS), jnp.float32)
    for slot in range(index.shape[0]):
        coefficient += jnp.where(
            adapter == index[slot : slot + 1, :], weight[slot : slot + 1, :], 0.0
        )
    coefficient = coefficient.T

    def of_segment(table):
        rows = table[...].astype(jnp.float32)
        return jnp.where(
            positions < first, rows[0:1], jnp.where(positions < second, rows[1:2], rows[2:3])
        )

    loads[0].wait()
    floats = latents_in[...].astype(jnp.float32)
    center = jnp.mean(floats, axis=1, keepdims=True)
    spread = floats - center
    variance = jnp.mean(spread * spread, axis=1, keepdims=True)
    normed = spread * (1.0 / jnp.sqrt(variance + epsilon))
    modulated = ((1.0 + of_segment(scale)) * normed + of_segment(shift)).astype(jnp.bfloat16)
    loads[1].wait()
    low_rank = jnp.dot(modulated, down_in[...], preferred_element_type=jnp.float32)
    scaled = (low_rank * coefficient).astype(jnp.bfloat16)
    for load in loads[2:]:
        load.wait()
    sends = []
    for chip in range(CHIPS):
        main, shared, row = heads_of(chip)
        stage[chip, 0:ROWS] = query_in[:, columns(main)]
        stage[chip, ROWS:Q_ROWS] = query_in[row : row + HALF, columns(shared)]
        stage[chip, K_AT : K_AT + ROWS] = key_in[:, columns(main)]
        stage[chip, K_AT + ROWS : V_AT] = key_in[:, columns(shared)]
        for head, at in ((main, V_AT), (shared, V_AT + ROWS)):
            update = jnp.dot(scaled, up_in[:, columns(head)], preferred_element_type=jnp.float32)
            mixed = value_in[:, columns(head)].astype(jnp.float32) + update
            stage[chip, at : at + ROWS] = mixed.astype(jnp.bfloat16)
        copy = pltpu.make_async_copy(stage.at[chip], send.at[chip], out_sems.at[chip])
        copy.start()
        sends.append(copy)
    for copy in sends:
        copy.wait()


def attend_kernel(
    lengths, own, peer, out, main_queries, shared_queries, keys, values, sems
):
    own_blocks, peer_blocks = pl.ds(0, CHIPS), pl.ds(CHIPS, CHIPS)
    low_lanes = slice(0, HEAD_DIM)
    copies = []
    for slot in range(2):
        k_at, v_at = pl.ds(K_AT + slot * ROWS, ROWS), pl.ds(V_AT + slot * ROWS, ROWS)
        if slot == 0:
            pairs = [(own.at[:, 0:ROWS], main_queries.at[:, :, low_lanes])]
        else:
            pairs = [(own.at[:, ROWS:Q_ROWS], shared_queries.at[:, :, low_lanes])]
        for source, blocks in ((own, own_blocks), (peer, peer_blocks)):
            pairs.append((source.at[:, k_at], keys.at[slot, blocks, :, low_lanes]))
            pairs.append((source.at[:, v_at], values.at[slot, blocks, :, low_lanes]))
        group = [
            pltpu.make_async_copy(source, target, sems.at[slot * 5 + n])
            for n, (source, target) in enumerate(pairs)
        ]
        for copy in group:
            copy.start()
        copies.append(group)

    first = lengths[0, 0]
    second = first + lengths[0, 1]
    device = lax.axis_index("seq")
    core = lax.rem(device, 2)
    shared_row = lax.rem(lax.div(device, 2), 2) * HALF

    def segment_of(position):
        return (position >= first).astype(jnp.int32) + (position >= second).astype(jnp.int32)

    def query_features(source, first_row, rows):
        shape = (rows, HEAD_DIM)
        token = (2 * source + core) * ROWS + first_row
        segment = segment_of(token + lax.broadcasted_iota(jnp.int32, shape, 0))
        lane = lax.broadcasted_iota(jnp.int32, shape, 1)
        return jnp.where(lane == segment, 1.0, 0.0).astype(jnp.bfloat16)

    def key_features(token):
        shape = (ROWS, HEAD_DIM)
        segment = segment_of(token + lax.broadcasted_iota(jnp.int32, shape, 0))
        lane = lax.broadcasted_iota(jnp.int32, shape, 1)
        return jnp.where((lane == segment) | (lane >= 3), 0.0, mask_value).astype(jnp.bfloat16)

    ones = jnp.ones((ROWS, HEAD_DIM), jnp.bfloat16)

    def fill(source, _):
        main_queries[source, :, HEAD_DIM:] = query_features(source, 0, ROWS)
        shared_queries[source, :, HEAD_DIM:] = query_features(source, shared_row, HALF)
        for block, parity in ((source, core), (source + CHIPS, 1 - core)):
            features = key_features((2 * source + parity) * ROWS)
            for slot in range(2):
                keys[slot, block, :, HEAD_DIM:] = features
                values[slot, block, :, HEAD_DIM:] = ones
        return 0

    lax.fori_loop(0, CHIPS, fill, 0)

    def attend(slot, queries):
        def scores_of(step):
            tile = keys[slot, step * STEP : (step + 1) * STEP]
            return lax.dot_general(
                queries,
                tile.reshape(STEP * ROWS, 2 * HEAD_DIM),
                (((1,), (1,)), ((), ())),
                preferred_element_type=jnp.float32,
            )

        steps = BLOCKS // STEP
        scores = scores_of(0)
        largest = accum = None
        for step in range(steps):
            ahead = scores_of(step + 1) if step + 1 < steps else None
            top = jnp.max(scores, axis=1, keepdims=True)
            top = top if step == 0 else jnp.maximum(largest, top)
            expo = jnp.exp2((scores - top) * to_base2).astype(jnp.bfloat16)
            tile = values[slot, step * STEP : (step + 1) * STEP]
            part = jnp.dot(
                expo,
                tile.reshape(STEP * ROWS, 2 * HEAD_DIM),
                preferred_element_type=jnp.float32,
            )
            accum = part if step == 0 else accum * jnp.exp2((largest - top) * to_base2) + part
            largest, scores = top, ahead
        return (accum[:, 0:HEAD_DIM] / accum[:, HEAD_DIM:]).astype(jnp.bfloat16)

    for slot, queries, rows, lanes in (
        (0, main_queries, ROWS, slice(0, ROWS)),
        (1, shared_queries, HALF, slice(ROWS, Q_ROWS)),
    ):
        for copy in copies[slot]:
            copy.wait()
        sources = TILE // rows

        def visit(tile, _, slot=slot, queries=queries, rows=rows, lanes=lanes, sources=sources):
            at = pl.ds(tile * sources, sources)
            result = attend(slot, queries[at].reshape(TILE, 2 * HEAD_DIM))
            out[at, lanes] = result.reshape(sources, rows, HEAD_DIM)
            return 0

        lax.fori_loop(0, CHIPS // sources, visit, 0)


def restore_kernel(returned, out, sems):
    copies = []
    for chip in range(CHIPS):
        main, shared, row = heads_of(chip)
        for source, target in (
            (returned.at[chip, 0:ROWS], out.at[:, columns(main)]),
            (returned.at[chip, ROWS:Q_ROWS], out.at[row : row + HALF, columns(shared)]),
        ):
            copy = pltpu.make_async_copy(source, target, sems.at[len(copies)])
            copy.start()
            copies.append(copy)
    for copy in copies:
        copy.wait()


def body(
    latents,
    modulation_shift,
    modulation_scale,
    query,
    key,
    value,
    adapter_down_weight,
    adapter_up_weight,
    adapter_index,
    adapter_weight,
    sequence_length,
):
    same_core = [[2 * c + k for c in range(CHIPS)] for k in range(2)]
    vmem = pl.BlockSpec(memory_space=pltpu.VMEM)
    smem = pl.BlockSpec(memory_space=pltpu.SMEM)
    anywhere = pl.BlockSpec(memory_space=pl.ANY)
    params = pltpu.CompilerParams(vmem_limit_bytes=40 * 1024 * 1024)
    width = HEADS * HEAD_DIM
    wide, dma = jnp.bfloat16, pltpu.SemaphoreType.DMA

    send = pl.pallas_call(
        prepare_kernel,
        out_shape=jax.ShapeDtypeStruct((CHIPS, PIECE, HEAD_DIM), wide),
        in_specs=[smem, anywhere, vmem, vmem] + [anywhere] * 5 + [vmem, vmem],
        out_specs=anywhere,
        scratch_shapes=[
            pltpu.VMEM((ROWS, width), wide),
            pltpu.VMEM((ROWS, width), wide),
            pltpu.VMEM((ROWS, width), wide),
            pltpu.VMEM((ROWS, width), wide),
            pltpu.VMEM((width, ROWS), wide),
            pltpu.VMEM((ROWS, width), wide),
            pltpu.VMEM((CHIPS, PIECE, HEAD_DIM), wide),
            dma((6,)),
            dma((CHIPS,)),
        ],
        compiler_params=pltpu.CompilerParams(vmem_limit_bytes=60 * 1024 * 1024),
        name="prepare",
    )(
        sequence_length,
        latents[0],
        modulation_shift[0],
        modulation_scale[0],
        query[0],
        key[0],
        value[0],
        adapter_down_weight,
        adapter_up_weight,
        adapter_index[0].T,
        adapter_weight[0].T,
    )
    own = lax.all_to_all(
        send, "seq", split_axis=0, concat_axis=0, tiled=True, axis_index_groups=same_core
    )
    peer = lax.ppermute(own, "seq", [(d, d ^ 1) for d in range(2 * CHIPS)])
    attended = pl.pallas_call(
        attend_kernel,
        out_shape=jax.ShapeDtypeStruct((CHIPS, Q_ROWS, HEAD_DIM), wide),
        in_specs=[smem, vmem, vmem],
        out_specs=vmem,
        scratch_shapes=[
            pltpu.VMEM((CHIPS, ROWS, 2 * HEAD_DIM), wide),
            pltpu.VMEM((CHIPS, HALF, 2 * HEAD_DIM), wide),
            pltpu.VMEM((2, BLOCKS, ROWS, 2 * HEAD_DIM), wide),
            pltpu.VMEM((2, BLOCKS, ROWS, 2 * HEAD_DIM), wide),
            dma((10,)),
        ],
        compiler_params=params,
        name="attend",
    )(sequence_length, own, peer)
    returned = lax.all_to_all(
        attended, "seq", split_axis=0, concat_axis=0, tiled=True, axis_index_groups=same_core
    )
    restored = pl.pallas_call(
        restore_kernel,
        out_shape=jax.ShapeDtypeStruct((ROWS, width), wide),
        in_specs=[vmem],
        out_specs=anywhere,
        scratch_shapes=[dma((2 * CHIPS,))],
        compiler_params=params,
        name="restore",
    )(returned)
    return restored[None]


def solution(mesh):
    in_specs = (
        P("dp", "seq", None),
        P("dp", None, None),
        P("dp", None, None),
        P("dp", "seq", None),
        P("dp", "seq", None),
        P("dp", "seq", None),
        P(),
        P(),
        P("dp", "seq", None),
        P("dp", "seq", None),
        P("dp", None),
    )
    out_specs = P("dp", "seq", None)
    return jax.shard_map(body, mesh=mesh, in_specs=in_specs, out_specs=out_specs, check_vma=False)
```

```python
import functools
import math

import jax
import jax.numpy as jnp
from jax import lax
from jax.experimental import pallas as pl
from jax.experimental.pallas import tpu as pltpu
from jax.sharding import PartitionSpec as P

HEADS = 24
HEAD_DIM = 128
STYLE_ADAPTERS = 8
ADAPTER_RANK = 16
ROWS = 128
CHIPS = 16
PACK_TOKENS = 4096
BLOCKS = PACK_TOKENS // ROWS
HALF = ROWS // 2
Q_ROWS = ROWS + HALF
K_AT = Q_ROWS
V_AT = K_AT + 2 * ROWS
PIECE = V_AT + 2 * ROWS
KV_ROWS = 4 * ROWS
TILE = 512
TILES = CHIPS * Q_ROWS // TILE
STEP = 8
SAFE_LOW, SAFE_HIGH = 2.0**-60, 2.0**100

mask_value = -1e30
epsilon = 1e-06
to_base2 = math.log2(math.e) / math.sqrt(HEAD_DIM)


def heads_of(chip):
    trio = 3 * (chip // 2)
    if chip % 2 == 0:
        return trio, trio + 1, 0
    return trio + 2, trio + 1, HALF


def columns(head):
    return slice(head * HEAD_DIM, (head + 1) * HEAD_DIM)


def prepare_kernel(
    lengths, latents, shift, scale, query, key, value, down, up, index, weight, send,
    latents_in, query_in, key_in, value_in, down_in, up_in, stage, in_sems, out_sems,
):
    pairs = (
        (latents, latents_in),
        (down, down_in),
        (up, up_in),
        (value, value_in),
        (query, query_in),
        (key, key_in),
    )
    loads = [
        pltpu.make_async_copy(source, target, in_sems.at[n])
        for n, (source, target) in enumerate(pairs)
    ]
    for load in loads:
        load.start()
    first = lengths[0, 0]
    second = first + lengths[0, 1]
    start = lax.axis_index("seq") * ROWS
    shape = (ROWS, ROWS)
    adapter = lax.broadcasted_iota(jnp.int32, shape, 0) // ADAPTER_RANK
    coefficient = jnp.zeros(shape, jnp.float32)
    for slot in range(index.shape[0]):
        coefficient += jnp.where(
            adapter == index[slot : slot + 1, :], weight[slot : slot + 1, :], 0.0
        )
    coefficient = coefficient.T
    segments = shift.shape[0]
    token = start + lax.broadcasted_iota(jnp.int32, (ROWS, segments), 0)
    segment = (token >= first).astype(jnp.int32) + (token >= second).astype(jnp.int32)
    lane = lax.broadcasted_iota(jnp.int32, (ROWS, segments), 1)
    chosen = jnp.where(lane == segment, 1.0, 0.0).astype(jnp.bfloat16)

    width = latents_in.shape[1]
    wide = 512
    chunks = width // wide

    def lanes_of(chunk):
        return slice(chunk * wide, (chunk + 1) * wide)

    def folded(values):
        parts = [values[:, n * HEAD_DIM : (n + 1) * HEAD_DIM] for n in range(wide // HEAD_DIM)]
        return functools.reduce(jnp.add, parts)

    loads[0].wait()
    zeros = jnp.zeros((ROWS, HEAD_DIM), jnp.float32)
    sums = zeros
    for n in range(chunks):
        sums += folded(latents_in[:, lanes_of(n)].astype(jnp.float32))
    center = jnp.sum(sums, axis=1, keepdims=True) * (1.0 / width)
    sums = zeros
    for n in range(chunks):
        spread = latents_in[:, lanes_of(n)].astype(jnp.float32) - center
        sums += folded(spread * spread)
    variance = jnp.sum(sums, axis=1, keepdims=True) * (1.0 / width)
    inverse = 1.0 / jnp.sqrt(variance + epsilon)
    loads[1].wait()
    low_rank = zeros
    for n in range(chunks):
        lanes = lanes_of(n)
        normed = (latents_in[:, lanes].astype(jnp.float32) - center) * inverse
        scales = jnp.dot(chosen, scale[:, lanes], preferred_element_type=jnp.float32)
        shifts = jnp.dot(chosen, shift[:, lanes], preferred_element_type=jnp.float32)
        modulated = ((1.0 + scales) * normed + shifts).astype(jnp.bfloat16)
        low_rank += jnp.dot(modulated, down_in[lanes, :], preferred_element_type=jnp.float32)
    scaled = (low_rank * coefficient).astype(jnp.bfloat16)
    for load in loads[2:]:
        load.wait()
    trio = 3 * HEAD_DIM

    def post(chip):
        return pltpu.make_async_copy(stage.at[chip], send.at[chip], out_sems.at[chip])

    for pair in range(CHIPS // 2):
        lanes = slice(pair * trio, (pair + 1) * trio)
        update = jnp.dot(scaled, up_in[:, lanes], preferred_element_type=jnp.float32)
        mixed = value_in[:, lanes].astype(jnp.float32) + update
        turned = [mixed[:, columns(head)].T.astype(jnp.bfloat16) for head in range(3)]
        for side in range(2):
            main, shared, row = heads_of(side)
            main_at, shared_at = columns(3 * pair + main), columns(3 * pair + shared)
            chip = 2 * pair + side
            stage[chip, 0:ROWS] = query_in[:, main_at]
            stage[chip, ROWS:Q_ROWS] = query_in[row : row + HALF, shared_at]
            stage[chip, K_AT : K_AT + ROWS] = key_in[:, main_at]
            stage[chip, K_AT + ROWS : V_AT] = key_in[:, shared_at]
            stage[chip, V_AT : V_AT + ROWS] = turned[main]
            stage[chip, V_AT + ROWS : PIECE] = turned[shared]
            post(chip).start()
    for chip in range(CHIPS):
        post(chip).wait()


def nt(left, right):
    return lax.dot_general(
        left, right, (((1,), (1,)), ((), ())), preferred_element_type=jnp.float32
    )


class Attention:
    def __init__(self, lengths):
        self.first = lengths[0, 0]
        self.second = self.first + lengths[0, 1]
        device = lax.axis_index("seq")
        self.core = lax.rem(device, 2)
        self.shared_row = lax.rem(lax.div(device, 2), 2) * HALF

    def same_segment_lane(self, source, core):
        shape = (ROWS, HEAD_DIM)
        token = (2 * source + core) * ROWS + lax.broadcasted_iota(jnp.int32, shape, 0)
        segment = (token >= self.first).astype(jnp.int32)
        segment += (token >= self.second).astype(jnp.int32)
        lane = lax.broadcasted_iota(jnp.int32, shape, 1)
        return lane == segment, lane

    def key_mark(self, source, core):
        same, lane = self.same_segment_lane(source, core)
        return jnp.where(same | (lane >= 3), 0.0, mask_value).astype(jnp.bfloat16)

    def fill(self, own, queries, query_mark, key_marks, peer_marks):
        low, high = slice(0, HEAD_DIM), slice(HEAD_DIM, 2 * HEAD_DIM)
        main, shared = TILE // ROWS, TILE // HALF

        def visit(source, _):
            same, _ = self.same_segment_lane(source, self.core)
            query_mark[...] = jnp.where(same, 1.0, 0.0).astype(jnp.bfloat16)
            key_marks[source] = self.key_mark(source, self.core)
            peer_marks[source] = self.key_mark(source, 1 - self.core)
            tile = lax.div(source, main)
            rows = pl.ds(pl.multiple_of(lax.rem(source, main) * ROWS, ROWS), ROWS)
            queries[tile, rows, low] = own[source, 0:ROWS]
            queries[tile, rows, high] = query_mark[...]
            tile = CHIPS // main + lax.div(source, shared)
            rows = pl.ds(pl.multiple_of(lax.rem(source, shared) * HALF, HALF), HALF)
            queries[tile, rows, low] = own[source, ROWS:Q_ROWS]
            mark_rows = pl.ds(pl.multiple_of(self.shared_row, HALF), HALF)
            queries[tile, rows, high] = query_mark[mark_rows, :]
            return 0

        lax.fori_loop(0, CHIPS, visit, 0)

    def rows_of(self, tile):
        kind = (tile >= CHIPS * ROWS // TILE).astype(jnp.int32)
        key_rows = pl.ds(pl.multiple_of(K_AT + kind * ROWS, HALF), ROWS)
        value_rows = pl.ds(pl.multiple_of(V_AT + kind * ROWS, HALF), ROWS)
        return key_rows, value_rows

    def add(self, tile, queries, source, marks, weights, total, accum):
        key_rows, value_rows = self.rows_of(tile)
        steps, count = CHIPS // STEP, STEP * ROWS
        for step in range(steps + 1):
            if step < steps:
                blocks = slice(step * STEP, (step + 1) * STEP)
                key_tile = source[blocks, key_rows].reshape(count, HEAD_DIM)
                mark = marks[blocks].reshape(count, HEAD_DIM)
                scores = nt(jnp.concatenate([key_tile, mark], axis=1), queries)
                expo = jnp.exp2(scores * to_base2)
                sums = jnp.sum(expo.reshape(count // 8, 8, TILE), axis=0)
                total = sums if total is None else total + sums
                weights[step % 2] = expo.astype(jnp.bfloat16)
            if step > 0:
                start = (step - 1) * STEP
                value_tile = [source[start + n, value_rows] for n in range(STEP)]
                part = jnp.dot(
                    jnp.concatenate(value_tile, axis=1),
                    weights[(step - 1) % 2],
                    preferred_element_type=jnp.float32,
                )
                accum = part if accum is None else accum + part
        return total, accum


def own_kernel(lengths, own, accums, totals, queries, peer_marks, query_mark, key_marks, weights):
    attention = Attention(lengths)
    attention.fill(own, queries, query_mark, key_marks, peer_marks)

    def visit(tile, _):
        total, accum = attention.add(tile, queries[tile], own, key_marks, weights, None, None)
        accums[tile] = accum
        totals[tile] = total
        return 0

    lax.fori_loop(0, TILES, visit, 0)


def peer_kernel(
    lengths, own, peer, accums, totals, queries, key_marks, out, weights,
    results, largest_ref, total_ref, accum_ref,
):
    attention = Attention(lengths)
    other = 1 - attention.core

    def store(tile, accum, total):
        results[tile] = (accum * (1.0 / total)).T.astype(jnp.bfloat16)

    def visit(tile, _):
        total, accum = attention.add(
            tile, queries[tile], peer, key_marks, weights, totals[tile], accums[tile]
        )
        total = jnp.sum(total, axis=0, keepdims=True)
        store(tile, accum, total)

        safe = (jnp.max(total) < SAFE_HIGH) & (jnp.min(total) > SAFE_LOW)

        @pl.when(jnp.logical_not(safe))
        def _():
            key_rows, value_rows = attention.rows_of(tile)
            largest_ref[...] = jnp.full((1, TILE), mask_value, jnp.float32)
            total_ref[...] = jnp.zeros((1, TILE), jnp.float32)
            accum_ref[...] = jnp.zeros((HEAD_DIM, TILE), jnp.float32)
            for source, core in ((own, attention.core), (peer, other)):

                def block(index, _, source=source, core=core):
                    mark = attention.key_mark(index, core)
                    key_tile = jnp.concatenate([source[index, key_rows], mark], axis=1)
                    scores = nt(key_tile, queries[tile])
                    largest = largest_ref[...]
                    top = jnp.maximum(largest, jnp.max(scores, axis=0, keepdims=True))
                    rescale = jnp.exp2((largest - top) * to_base2)
                    expo = jnp.exp2((scores - top) * to_base2)
                    largest_ref[...] = top
                    total_ref[...] = total_ref[...] * rescale + jnp.sum(
                        expo, axis=0, keepdims=True
                    )
                    accum_ref[...] = accum_ref[...] * rescale + jnp.dot(
                        source[index, value_rows],
                        expo.astype(jnp.bfloat16),
                        preferred_element_type=jnp.float32,
                    )
                    return 0

                lax.fori_loop(0, CHIPS, block, 0)
            store(tile, accum_ref[...], total_ref[...])

        return 0

    lax.fori_loop(0, TILES, visit, 0)
    main = CHIPS * ROWS // TILE
    out[:, 0:ROWS] = results[0:main].reshape(CHIPS, ROWS, HEAD_DIM)
    out[:, ROWS:Q_ROWS] = results[main:TILES].reshape(CHIPS, HALF, HEAD_DIM)


def restore_kernel(returned, out, sems):
    copies = []
    for chip in range(CHIPS):
        main, shared, row = heads_of(chip)
        for source, target in (
            (returned.at[chip, 0:ROWS], out.at[:, columns(main)]),
            (returned.at[chip, ROWS:Q_ROWS], out.at[row : row + HALF, columns(shared)]),
        ):
            copy = pltpu.make_async_copy(source, target, sems.at[len(copies)])
            copy.start()
            copies.append(copy)
    for copy in copies:
        copy.wait()


def body(
    latents,
    modulation_shift,
    modulation_scale,
    query,
    key,
    value,
    adapter_down_weight,
    adapter_up_weight,
    adapter_index,
    adapter_weight,
    sequence_length,
):
    same_core = [[2 * c + k for c in range(CHIPS)] for k in range(2)]
    vmem = pl.BlockSpec(memory_space=pltpu.VMEM)
    smem = pl.BlockSpec(memory_space=pltpu.SMEM)
    anywhere = pl.BlockSpec(memory_space=pl.ANY)
    params = pltpu.CompilerParams(vmem_limit_bytes=36 * 1024 * 1024)
    width = HEADS * HEAD_DIM
    wide, dma = jnp.bfloat16, pltpu.SemaphoreType.DMA

    send = pl.pallas_call(
        prepare_kernel,
        out_shape=jax.ShapeDtypeStruct((CHIPS, PIECE, HEAD_DIM), wide),
        in_specs=[smem, anywhere, vmem, vmem] + [anywhere] * 5 + [vmem, vmem],
        out_specs=anywhere,
        scratch_shapes=[
            pltpu.VMEM((ROWS, width), wide),
            pltpu.VMEM((ROWS, width), wide),
            pltpu.VMEM((ROWS, width), wide),
            pltpu.VMEM((ROWS, width), wide),
            pltpu.VMEM((width, ROWS), wide),
            pltpu.VMEM((ROWS, width), wide),
            pltpu.VMEM((CHIPS, PIECE, HEAD_DIM), wide),
            dma((6,)),
            dma((CHIPS,)),
        ],
        compiler_params=pltpu.CompilerParams(vmem_limit_bytes=60 * 1024 * 1024),
        name="prepare",
    )(
        sequence_length,
        latents[0],
        modulation_shift[0],
        modulation_scale[0],
        query[0],
        key[0],
        value[0],
        adapter_down_weight,
        adapter_up_weight,
        adapter_index[0].T,
        adapter_weight[0].T,
    )
    own = lax.all_to_all(
        send, "seq", split_axis=0, concat_axis=0, tiled=True, axis_index_groups=same_core
    )
    peer = lax.ppermute(own, "seq", [(d, d ^ 1) for d in range(2 * CHIPS)])
    pairs = TILES * TILE * PACK_TOKENS // 2
    cost = pl.CostEstimate(
        flops=6 * HEAD_DIM * pairs, bytes_accessed=4 << 20, transcendentals=pairs
    )
    marks = pltpu.VMEM((CHIPS, ROWS, HEAD_DIM), wide)
    weights = pltpu.VMEM((2, STEP * ROWS, TILE), wide)
    state = pl.pallas_call(
        own_kernel,
        out_shape=[
            jax.ShapeDtypeStruct((TILES, HEAD_DIM, TILE), jnp.float32),
            jax.ShapeDtypeStruct((TILES, 8, TILE), jnp.float32),
            jax.ShapeDtypeStruct((TILES, TILE, 2 * HEAD_DIM), wide),
            jax.ShapeDtypeStruct((CHIPS, ROWS, HEAD_DIM), wide),
        ],
        in_specs=[smem, vmem],
        out_specs=[vmem] * 4,
        scratch_shapes=[pltpu.VMEM((ROWS, HEAD_DIM), wide), marks, weights],
        compiler_params=params,
        cost_estimate=cost,
        name="attend_own",
    )(sequence_length, own)
    attended = pl.pallas_call(
        peer_kernel,
        out_shape=jax.ShapeDtypeStruct((CHIPS, Q_ROWS, HEAD_DIM), wide),
        in_specs=[smem] + [vmem] * 6,
        out_specs=vmem,
        scratch_shapes=[
            weights,
            pltpu.VMEM((TILES, TILE, HEAD_DIM), wide),
            pltpu.VMEM((1, TILE), jnp.float32),
            pltpu.VMEM((1, TILE), jnp.float32),
            pltpu.VMEM((HEAD_DIM, TILE), jnp.float32),
        ],
        compiler_params=params,
        cost_estimate=cost,
        name="attend_peer",
    )(sequence_length, own, peer, *state)
    returned = lax.all_to_all(
        attended, "seq", split_axis=0, concat_axis=0, tiled=True, axis_index_groups=same_core
    )
    restored = pl.pallas_call(
        restore_kernel,
        out_shape=jax.ShapeDtypeStruct((ROWS, width), wide),
        in_specs=[vmem],
        out_specs=anywhere,
        scratch_shapes=[dma((2 * CHIPS,))],
        compiler_params=params,
        name="restore",
    )(returned)
    return restored[None]


def solution(mesh):
    in_specs = (
        P("dp", "seq", None),
        P("dp", None, None),
        P("dp", None, None),
        P("dp", "seq", None),
        P("dp", "seq", None),
        P("dp", "seq", None),
        P(),
        P(),
        P("dp", "seq", None),
        P("dp", "seq", None),
        P("dp", None),
    )
    out_specs = P("dp", "seq", None)
    return jax.shard_map(body, mesh=mesh, in_specs=in_specs, out_specs=out_specs, check_vma=False)
```

```python
import functools
import math

import jax
import jax.numpy as jnp
from jax import lax
from jax.experimental import pallas as pl
from jax.experimental.pallas import tpu as pltpu
from jax.sharding import PartitionSpec as P

HEADS = 24
HEAD_DIM = 128
STYLE_ADAPTERS = 8
ADAPTER_RANK = 16
ROWS = 128
CHIPS = 16
PACK_TOKENS = 4096
BLOCKS = PACK_TOKENS // ROWS
HALF = ROWS // 2
Q_ROWS = ROWS + HALF
K_AT = Q_ROWS
V_AT = K_AT + 2 * ROWS
PIECE = V_AT + 2 * ROWS
KV_ROWS = 4 * ROWS
TILE = 512
TILES = CHIPS * Q_ROWS // TILE
STEP = 8
SAFE_LOW, SAFE_HIGH = 2.0**-60, 2.0**100

mask_value = -1e30
epsilon = 1e-06
to_base2 = math.log2(math.e) / math.sqrt(HEAD_DIM)


def heads_of(chip):
    trio = 3 * (chip // 2)
    if chip % 2 == 0:
        return trio, trio + 1, 0
    return trio + 2, trio + 1, HALF


def columns(head):
    return slice(head * HEAD_DIM, (head + 1) * HEAD_DIM)


def prepare_kernel(
    lengths, latents, shift, scale, query, key, value, down, up, index, weight, send,
    latents_in, query_in, key_in, value_in, down_in, up_in, in_sems,
):
    pairs = (
        (latents, latents_in),
        (down, down_in),
        (up, up_in),
        (value, value_in),
        (query, query_in),
        (key, key_in),
    )
    loads = [
        pltpu.make_async_copy(source, target, in_sems.at[n])
        for n, (source, target) in enumerate(pairs)
    ]
    for load in loads:
        load.start()
    first = lengths[0, 0]
    second = first + lengths[0, 1]
    start = lax.axis_index("seq") * ROWS
    shape = (ROWS, ROWS)
    adapter = lax.broadcasted_iota(jnp.int32, shape, 0) // ADAPTER_RANK
    coefficient = jnp.zeros(shape, jnp.float32)
    for slot in range(index.shape[0]):
        coefficient += jnp.where(
            adapter == index[slot : slot + 1, :], weight[slot : slot + 1, :], 0.0
        )
    coefficient = coefficient.T
    segments = shift.shape[0]
    token = start + lax.broadcasted_iota(jnp.int32, (ROWS, segments), 0)
    segment = (token >= first).astype(jnp.int32) + (token >= second).astype(jnp.int32)
    lane = lax.broadcasted_iota(jnp.int32, (ROWS, segments), 1)
    chosen = jnp.where(lane == segment, 1.0, 0.0).astype(jnp.bfloat16)

    width = latents_in.shape[1]
    wide = 512
    chunks = width // wide

    def lanes_of(chunk):
        return slice(chunk * wide, (chunk + 1) * wide)

    def folded(values):
        parts = [values[:, n * HEAD_DIM : (n + 1) * HEAD_DIM] for n in range(wide // HEAD_DIM)]
        return functools.reduce(jnp.add, parts)

    loads[0].wait()
    zeros = jnp.zeros((ROWS, HEAD_DIM), jnp.float32)
    sums = zeros
    for n in range(chunks):
        sums += folded(latents_in[:, lanes_of(n)].astype(jnp.float32))
    center = jnp.sum(sums, axis=1, keepdims=True) * (1.0 / width)
    sums = zeros
    for n in range(chunks):
        spread = latents_in[:, lanes_of(n)].astype(jnp.float32) - center
        sums += folded(spread * spread)
    variance = jnp.sum(sums, axis=1, keepdims=True) * (1.0 / width)
    inverse = 1.0 / jnp.sqrt(variance + epsilon)
    loads[1].wait()
    low_rank = zeros
    for n in range(chunks):
        lanes = lanes_of(n)
        normed = (latents_in[:, lanes].astype(jnp.float32) - center) * inverse
        scales = jnp.dot(chosen, scale[:, lanes], preferred_element_type=jnp.float32)
        shifts = jnp.dot(chosen, shift[:, lanes], preferred_element_type=jnp.float32)
        modulated = ((1.0 + scales) * normed + shifts).astype(jnp.bfloat16)
        low_rank += jnp.dot(modulated, down_in[lanes, :], preferred_element_type=jnp.float32)
    scaled = (low_rank * coefficient).astype(jnp.bfloat16)
    for load in loads[2:]:
        load.wait()
    trio = 3 * HEAD_DIM

    for pair in range(CHIPS // 2):
        lanes = slice(pair * trio, (pair + 1) * trio)
        update = jnp.dot(scaled, up_in[:, lanes], preferred_element_type=jnp.float32)
        mixed = value_in[:, lanes].astype(jnp.float32) + update
        turned = [mixed[:, columns(head)].T.astype(jnp.bfloat16) for head in range(3)]
        for side in range(2):
            main, shared, row = heads_of(side)
            main_at, shared_at = columns(3 * pair + main), columns(3 * pair + shared)
            chip = 2 * pair + side
            send[chip, 0:ROWS] = query_in[:, main_at]
            send[chip, ROWS:Q_ROWS] = query_in[row : row + HALF, shared_at]
            send[chip, K_AT : K_AT + ROWS] = key_in[:, main_at]
            send[chip, K_AT + ROWS : V_AT] = key_in[:, shared_at]
            send[chip, V_AT : V_AT + ROWS] = turned[main]
            send[chip, V_AT + ROWS : PIECE] = turned[shared]


def nt(left, right):
    return lax.dot_general(
        left, right, (((1,), (1,)), ((), ())), preferred_element_type=jnp.float32
    )


class Attention:
    def __init__(self, lengths):
        self.first = lengths[0, 0]
        self.second = self.first + lengths[0, 1]
        device = lax.axis_index("seq")
        self.core = lax.rem(device, 2)
        self.shared_row = lax.rem(lax.div(device, 2), 2) * HALF

    def same_segment_lane(self, source, core):
        shape = (ROWS, HEAD_DIM)
        token = (2 * source + core) * ROWS + lax.broadcasted_iota(jnp.int32, shape, 0)
        segment = (token >= self.first).astype(jnp.int32)
        segment += (token >= self.second).astype(jnp.int32)
        lane = lax.broadcasted_iota(jnp.int32, shape, 1)
        return lane == segment, lane

    def key_mark(self, source, core):
        same, lane = self.same_segment_lane(source, core)
        return jnp.where(same | (lane >= 3), 0.0, mask_value).astype(jnp.bfloat16)

    def fill(self, own, queries, query_mark, key_marks, peer_marks):
        low, high = slice(0, HEAD_DIM), slice(HEAD_DIM, 2 * HEAD_DIM)
        main, shared = TILE // ROWS, TILE // HALF

        def visit(source, _):
            same, _ = self.same_segment_lane(source, self.core)
            query_mark[...] = jnp.where(same, 1.0, 0.0).astype(jnp.bfloat16)
            key_marks[source] = self.key_mark(source, self.core)
            peer_marks[source] = self.key_mark(source, 1 - self.core)
            tile = lax.div(source, main)
            rows = pl.ds(pl.multiple_of(lax.rem(source, main) * ROWS, ROWS), ROWS)
            queries[tile, rows, low] = own[source, 0:ROWS]
            queries[tile, rows, high] = query_mark[...]
            tile = CHIPS // main + lax.div(source, shared)
            rows = pl.ds(pl.multiple_of(lax.rem(source, shared) * HALF, HALF), HALF)
            queries[tile, rows, low] = own[source, ROWS:Q_ROWS]
            mark_rows = pl.ds(pl.multiple_of(self.shared_row, HALF), HALF)
            queries[tile, rows, high] = query_mark[mark_rows, :]
            return 0

        lax.fori_loop(0, CHIPS, visit, 0)

    def rows_of(self, tile):
        kind = (tile >= CHIPS * ROWS // TILE).astype(jnp.int32)
        key_rows = pl.ds(pl.multiple_of(K_AT + kind * ROWS, HALF), ROWS)
        value_rows = pl.ds(pl.multiple_of(V_AT + kind * ROWS, HALF), ROWS)
        return key_rows, value_rows

    def add(self, tile, queries, source, marks, weights, total, accum):
        key_rows, value_rows = self.rows_of(tile)
        steps, count = CHIPS // STEP, STEP * ROWS
        for step in range(steps + 1):
            if step < steps:
                blocks = slice(step * STEP, (step + 1) * STEP)
                key_tile = source[blocks, key_rows].reshape(count, HEAD_DIM)
                mark = marks[blocks].reshape(count, HEAD_DIM)
                scores = nt(jnp.concatenate([key_tile, mark], axis=1), queries)
                expo = jnp.exp2(scores * to_base2)
                sums = jnp.sum(expo.reshape(count // 8, 8, TILE), axis=0)
                total = sums if total is None else total + sums
                weights[step % 2] = expo.astype(jnp.bfloat16)
            if step > 0:
                start = (step - 1) * STEP
                value_tile = [source[start + n, value_rows] for n in range(STEP)]
                part = jnp.dot(
                    jnp.concatenate(value_tile, axis=1),
                    weights[(step - 1) % 2],
                    preferred_element_type=jnp.float32,
                )
                accum = part if accum is None else accum + part
        return total, accum


def own_kernel(lengths, own, accums, totals, queries, peer_marks, query_mark, key_marks, weights):
    attention = Attention(lengths)
    attention.fill(own, queries, query_mark, key_marks, peer_marks)

    def visit(tile, _):
        total, accum = attention.add(tile, queries[tile], own, key_marks, weights, None, None)
        accums[tile] = accum
        totals[tile] = total
        return 0

    lax.fori_loop(0, TILES, visit, 0)


def peer_kernel(
    lengths, own, peer, accums, totals, queries, key_marks, out, weights,
    results, largest_ref, total_ref, accum_ref,
):
    attention = Attention(lengths)
    other = 1 - attention.core

    def store(tile, accum, total):
        results[tile] = (accum * (1.0 / total)).T.astype(jnp.bfloat16)

    def visit(tile, _):
        total, accum = attention.add(
            tile, queries[tile], peer, key_marks, weights, totals[tile], accums[tile]
        )
        total = jnp.sum(total, axis=0, keepdims=True)
        store(tile, accum, total)

        safe = (jnp.max(total) < SAFE_HIGH) & (jnp.min(total) > SAFE_LOW)

        @pl.when(jnp.logical_not(safe))
        def _():
            key_rows, value_rows = attention.rows_of(tile)
            largest_ref[...] = jnp.full((1, TILE), mask_value, jnp.float32)
            total_ref[...] = jnp.zeros((1, TILE), jnp.float32)
            accum_ref[...] = jnp.zeros((HEAD_DIM, TILE), jnp.float32)
            for source, core in ((own, attention.core), (peer, other)):

                def block(index, _, source=source, core=core):
                    mark = attention.key_mark(index, core)
                    key_tile = jnp.concatenate([source[index, key_rows], mark], axis=1)
                    scores = nt(key_tile, queries[tile])
                    largest = largest_ref[...]
                    top = jnp.maximum(largest, jnp.max(scores, axis=0, keepdims=True))
                    rescale = jnp.exp2((largest - top) * to_base2)
                    expo = jnp.exp2((scores - top) * to_base2)
                    largest_ref[...] = top
                    total_ref[...] = total_ref[...] * rescale + jnp.sum(
                        expo, axis=0, keepdims=True
                    )
                    accum_ref[...] = accum_ref[...] * rescale + jnp.dot(
                        source[index, value_rows],
                        expo.astype(jnp.bfloat16),
                        preferred_element_type=jnp.float32,
                    )
                    return 0

                lax.fori_loop(0, CHIPS, block, 0)
            store(tile, accum_ref[...], total_ref[...])

        return 0

    lax.fori_loop(0, TILES, visit, 0)
    main = CHIPS * ROWS // TILE
    out[:, 0:ROWS] = results[0:main].reshape(CHIPS, ROWS, HEAD_DIM)
    out[:, ROWS:Q_ROWS] = results[main:TILES].reshape(CHIPS, HALF, HEAD_DIM)


def restore_kernel(returned, out, sems):
    copies = []
    for chip in range(CHIPS):
        main, shared, row = heads_of(chip)
        for source, target in (
            (returned.at[chip, 0:ROWS], out.at[:, columns(main)]),
            (returned.at[chip, ROWS:Q_ROWS], out.at[row : row + HALF, columns(shared)]),
        ):
            copy = pltpu.make_async_copy(source, target, sems.at[len(copies)])
            copy.start()
            copies.append(copy)
    for copy in copies:
        copy.wait()


def body(
    latents,
    modulation_shift,
    modulation_scale,
    query,
    key,
    value,
    adapter_down_weight,
    adapter_up_weight,
    adapter_index,
    adapter_weight,
    sequence_length,
):
    same_core = [[2 * c + k for c in range(CHIPS)] for k in range(2)]
    vmem = pl.BlockSpec(memory_space=pltpu.VMEM)
    smem = pl.BlockSpec(memory_space=pltpu.SMEM)
    anywhere = pl.BlockSpec(memory_space=pl.ANY)
    params = pltpu.CompilerParams(vmem_limit_bytes=36 * 1024 * 1024)
    width = HEADS * HEAD_DIM
    wide, dma = jnp.bfloat16, pltpu.SemaphoreType.DMA

    send = pl.pallas_call(
        prepare_kernel,
        out_shape=jax.ShapeDtypeStruct((CHIPS, PIECE, HEAD_DIM), wide),
        in_specs=[smem, anywhere, vmem, vmem] + [anywhere] * 5 + [vmem, vmem],
        out_specs=vmem,
        scratch_shapes=[
            pltpu.VMEM((ROWS, width), wide),
            pltpu.VMEM((ROWS, width), wide),
            pltpu.VMEM((ROWS, width), wide),
            pltpu.VMEM((ROWS, width), wide),
            pltpu.VMEM((width, ROWS), wide),
            pltpu.VMEM((ROWS, width), wide),
            dma((6,)),
        ],
        compiler_params=params,
        name="prepare",
    )(
        *(
            pltpu.with_memory_space_constraint(operand, pltpu.HBM)
            for operand in (
                sequence_length,
                latents[0],
                modulation_shift[0],
                modulation_scale[0],
                query[0],
                key[0],
                value[0],
                adapter_down_weight,
                adapter_up_weight,
                adapter_index[0].T,
                adapter_weight[0].T,
            )
        )
    )
    own = lax.all_to_all(
        send, "seq", split_axis=0, concat_axis=0, tiled=True, axis_index_groups=same_core
    )
    peer = lax.ppermute(own, "seq", [(d, d ^ 1) for d in range(2 * CHIPS)])
    pairs = TILES * TILE * PACK_TOKENS // 2
    cost = pl.CostEstimate(
        flops=6 * HEAD_DIM * pairs, bytes_accessed=4 << 20, transcendentals=pairs
    )
    marks = pltpu.VMEM((CHIPS, ROWS, HEAD_DIM), wide)
    weights = pltpu.VMEM((2, STEP * ROWS, TILE), wide)
    state = pl.pallas_call(
        own_kernel,
        out_shape=[
            jax.ShapeDtypeStruct((TILES, HEAD_DIM, TILE), jnp.float32),
            jax.ShapeDtypeStruct((TILES, 8, TILE), jnp.float32),
            jax.ShapeDtypeStruct((TILES, TILE, 2 * HEAD_DIM), wide),
            jax.ShapeDtypeStruct((CHIPS, ROWS, HEAD_DIM), wide),
        ],
        in_specs=[smem, vmem],
        out_specs=[vmem] * 4,
        scratch_shapes=[pltpu.VMEM((ROWS, HEAD_DIM), wide), marks, weights],
        compiler_params=params,
        cost_estimate=cost,
        name="attend_own",
    )(sequence_length, own)
    attended = pl.pallas_call(
        peer_kernel,
        out_shape=jax.ShapeDtypeStruct((CHIPS, Q_ROWS, HEAD_DIM), wide),
        in_specs=[smem] + [vmem] * 6,
        out_specs=vmem,
        scratch_shapes=[
            weights,
            pltpu.VMEM((TILES, TILE, HEAD_DIM), wide),
            pltpu.VMEM((1, TILE), jnp.float32),
            pltpu.VMEM((1, TILE), jnp.float32),
            pltpu.VMEM((HEAD_DIM, TILE), jnp.float32),
        ],
        compiler_params=params,
        cost_estimate=cost,
        name="attend_peer",
    )(sequence_length, own, peer, *state)
    returned = lax.all_to_all(
        attended, "seq", split_axis=0, concat_axis=0, tiled=True, axis_index_groups=same_core
    )
    restored = pl.pallas_call(
        restore_kernel,
        out_shape=jax.ShapeDtypeStruct((ROWS, width), wide),
        in_specs=[vmem],
        out_specs=anywhere,
        scratch_shapes=[dma((2 * CHIPS,))],
        compiler_params=params,
        name="restore",
    )(returned)
    return restored[None]


def solution(mesh):
    in_specs = (
        P("dp", "seq", None),
        P("dp", None, None),
        P("dp", None, None),
        P("dp", "seq", None),
        P("dp", "seq", None),
        P("dp", "seq", None),
        P(),
        P(),
        P("dp", "seq", None),
        P("dp", "seq", None),
        P("dp", None),
    )
    out_specs = P("dp", "seq", None)
    return jax.shard_map(body, mesh=mesh, in_specs=in_specs, out_specs=out_specs, check_vma=False)
```

```python
import functools
import math

import jax
import jax.numpy as jnp
from jax import lax
from jax.experimental import pallas as pl
from jax.experimental.pallas import tpu as pltpu
from jax.sharding import PartitionSpec as P

HEADS = 24
HEAD_DIM = 128
STYLE_ADAPTERS = 8
ADAPTER_RANK = 16
ROWS = 128
CHIPS = 16
PACK_TOKENS = 4096
BLOCKS = PACK_TOKENS // ROWS
HALF = ROWS // 2
Q_ROWS = ROWS + HALF
K_AT = Q_ROWS
V_AT = K_AT + 2 * ROWS
PIECE = V_AT + 2 * ROWS
KV_ROWS = 4 * ROWS
TILE = 1024
TILES = CHIPS * Q_ROWS // TILE
STEP = 8
SAFE_LOW, SAFE_HIGH = 2.0**-60, 2.0**100

mask_value = -1e30
epsilon = 1e-06
to_base2 = math.log2(math.e) / math.sqrt(HEAD_DIM)


def heads_of(chip):
    trio = 3 * (chip // 2)
    if chip % 2 == 0:
        return trio, trio + 1, 0
    return trio + 2, trio + 1, HALF


def columns(head):
    return slice(head * HEAD_DIM, (head + 1) * HEAD_DIM)


def prepare_kernel(
    lengths, latents, shift, scale, query, key, value, down, up, index, weight, send,
    latents_in, query_in, key_in, value_in, down_in, up_in, in_sems,
):
    pairs = (
        (latents, latents_in),
        (down, down_in),
        (up, up_in),
        (value, value_in),
        (query, query_in),
        (key, key_in),
    )
    loads = [
        pltpu.make_async_copy(source, target, in_sems.at[n])
        for n, (source, target) in enumerate(pairs)
    ]
    for load in loads:
        load.start()
    first = lengths[0, 0]
    second = first + lengths[0, 1]
    start = lax.axis_index("seq") * ROWS
    shape = (ROWS, ROWS)
    adapter = lax.broadcasted_iota(jnp.int32, shape, 0) // ADAPTER_RANK
    coefficient = jnp.zeros(shape, jnp.float32)
    for slot in range(index.shape[0]):
        coefficient += jnp.where(
            adapter == index[slot : slot + 1, :], weight[slot : slot + 1, :], 0.0
        )
    coefficient = coefficient.T
    segments = shift.shape[0]
    token = start + lax.broadcasted_iota(jnp.int32, (ROWS, segments), 0)
    segment = (token >= first).astype(jnp.int32) + (token >= second).astype(jnp.int32)
    lane = lax.broadcasted_iota(jnp.int32, (ROWS, segments), 1)
    chosen = jnp.where(lane == segment, 1.0, 0.0).astype(jnp.bfloat16)

    width = latents_in.shape[1]
    wide = 512
    chunks = width // wide

    def lanes_of(chunk):
        return slice(chunk * wide, (chunk + 1) * wide)

    def folded(values):
        parts = [values[:, n * HEAD_DIM : (n + 1) * HEAD_DIM] for n in range(wide // HEAD_DIM)]
        return functools.reduce(jnp.add, parts)

    loads[0].wait()
    zeros = jnp.zeros((ROWS, HEAD_DIM), jnp.float32)
    sums = zeros
    for n in range(chunks):
        sums += folded(latents_in[:, lanes_of(n)].astype(jnp.float32))
    center = jnp.sum(sums, axis=1, keepdims=True) * (1.0 / width)
    sums = zeros
    for n in range(chunks):
        spread = latents_in[:, lanes_of(n)].astype(jnp.float32) - center
        sums += folded(spread * spread)
    variance = jnp.sum(sums, axis=1, keepdims=True) * (1.0 / width)
    inverse = 1.0 / jnp.sqrt(variance + epsilon)
    loads[1].wait()
    low_rank = zeros
    for n in range(chunks):
        lanes = lanes_of(n)
        normed = (latents_in[:, lanes].astype(jnp.float32) - center) * inverse
        scales = jnp.dot(chosen, scale[:, lanes], preferred_element_type=jnp.float32)
        shifts = jnp.dot(chosen, shift[:, lanes], preferred_element_type=jnp.float32)
        modulated = ((1.0 + scales) * normed + shifts).astype(jnp.bfloat16)
        low_rank += jnp.dot(modulated, down_in[lanes, :], preferred_element_type=jnp.float32)
    scaled = (low_rank * coefficient).astype(jnp.bfloat16)
    for load in loads[2:]:
        load.wait()
    trio = 3 * HEAD_DIM

    for pair in range(CHIPS // 2):
        lanes = slice(pair * trio, (pair + 1) * trio)
        update = jnp.dot(scaled, up_in[:, lanes], preferred_element_type=jnp.float32)
        mixed = value_in[:, lanes].astype(jnp.float32) + update
        turned = [mixed[:, columns(head)].T.astype(jnp.bfloat16) for head in range(3)]
        for side in range(2):
            main, shared, row = heads_of(side)
            main_at, shared_at = columns(3 * pair + main), columns(3 * pair + shared)
            chip = 2 * pair + side
            send[chip, 0:ROWS] = query_in[:, main_at]
            send[chip, ROWS:Q_ROWS] = query_in[row : row + HALF, shared_at]
            send[chip, K_AT : K_AT + ROWS] = key_in[:, main_at]
            send[chip, K_AT + ROWS : V_AT] = key_in[:, shared_at]
            send[chip, V_AT : V_AT + ROWS] = turned[main]
            send[chip, V_AT + ROWS : PIECE] = turned[shared]


def nt(left, right):
    return lax.dot_general(
        left, right, (((1,), (1,)), ((), ())), preferred_element_type=jnp.float32
    )


class Attention:
    def __init__(self, lengths):
        self.first = lengths[0, 0]
        self.second = self.first + lengths[0, 1]
        device = lax.axis_index("seq")
        self.core = lax.rem(device, 2)
        self.shared_row = lax.rem(lax.div(device, 2), 2) * HALF

    def same_segment_lane(self, source, core):
        shape = (ROWS, HEAD_DIM)
        token = (2 * source + core) * ROWS + lax.broadcasted_iota(jnp.int32, shape, 0)
        segment = (token >= self.first).astype(jnp.int32)
        segment += (token >= self.second).astype(jnp.int32)
        lane = lax.broadcasted_iota(jnp.int32, shape, 1)
        return lane == segment, lane

    def key_mark(self, source, core):
        same, lane = self.same_segment_lane(source, core)
        return jnp.where(same | (lane >= 3), 0.0, mask_value).astype(jnp.bfloat16)

    def fill(self, own, queries, query_mark, key_marks, peer_marks):
        low, high = slice(0, HEAD_DIM), slice(HEAD_DIM, 2 * HEAD_DIM)
        main, shared = TILE // ROWS, TILE // HALF

        def visit(source, _):
            same, _ = self.same_segment_lane(source, self.core)
            query_mark[...] = jnp.where(same, 1.0, 0.0).astype(jnp.bfloat16)
            key_marks[source] = self.key_mark(source, self.core)
            peer_marks[source] = self.key_mark(source, 1 - self.core)
            tile = lax.div(source, main)
            rows = pl.ds(pl.multiple_of(lax.rem(source, main) * ROWS, ROWS), ROWS)
            queries[tile, rows, low] = own[source, 0:ROWS]
            queries[tile, rows, high] = query_mark[...]
            tile = CHIPS // main + lax.div(source, shared)
            rows = pl.ds(pl.multiple_of(lax.rem(source, shared) * HALF, HALF), HALF)
            queries[tile, rows, low] = own[source, ROWS:Q_ROWS]
            mark_rows = pl.ds(pl.multiple_of(self.shared_row, HALF), HALF)
            queries[tile, rows, high] = query_mark[mark_rows, :]
            return 0

        lax.fori_loop(0, CHIPS, visit, 0)

    def rows_of(self, tile):
        kind = (tile >= CHIPS * ROWS // TILE).astype(jnp.int32)
        key_rows = pl.ds(pl.multiple_of(K_AT + kind * ROWS, HALF), ROWS)
        value_rows = pl.ds(pl.multiple_of(V_AT + kind * ROWS, HALF), ROWS)
        return key_rows, value_rows

    def add(self, tile, queries, source, marks, weights, total, accum):
        key_rows, value_rows = self.rows_of(tile)
        steps, count = CHIPS // STEP, STEP * ROWS
        for step in range(steps + 1):
            if step < steps:
                blocks = slice(step * STEP, (step + 1) * STEP)
                key_tile = source[blocks, key_rows].reshape(count, HEAD_DIM)
                mark = marks[blocks].reshape(count, HEAD_DIM)
                scores = nt(jnp.concatenate([key_tile, mark], axis=1), queries)
                expo = jnp.exp2(scores * to_base2)
                sums = jnp.sum(expo.reshape(count // 8, 8, TILE), axis=0)
                total = sums if total is None else total + sums
                weights[step % 2] = expo.astype(jnp.bfloat16)
            if step > 0:
                start = (step - 1) * STEP
                value_tile = [source[start + n, value_rows] for n in range(STEP)]
                part = jnp.dot(
                    jnp.concatenate(value_tile, axis=1),
                    weights[(step - 1) % 2],
                    preferred_element_type=jnp.float32,
                )
                accum = part if accum is None else accum + part
        return total, accum


def own_kernel(lengths, own, accums, totals, queries, peer_marks, query_mark, key_marks, weights):
    attention = Attention(lengths)
    attention.fill(own, queries, query_mark, key_marks, peer_marks)

    def visit(tile, _):
        total, accum = attention.add(tile, queries[tile], own, key_marks, weights, None, None)
        accums[tile] = accum
        totals[tile] = total
        return 0

    lax.fori_loop(0, TILES, visit, 0)


def peer_kernel(
    lengths, own, peer, accums, totals, queries, key_marks, out, weights,
    results, largest_ref, total_ref, accum_ref,
):
    attention = Attention(lengths)
    other = 1 - attention.core

    def store(tile, accum, total):
        results[tile] = (accum * (1.0 / total)).T.astype(jnp.bfloat16)

    def visit(tile, _):
        total, accum = attention.add(
            tile, queries[tile], peer, key_marks, weights, totals[tile], accums[tile]
        )
        total = jnp.sum(total, axis=0, keepdims=True)
        store(tile, accum, total)

        safe = (jnp.max(total) < SAFE_HIGH) & (jnp.min(total) > SAFE_LOW)

        @pl.when(jnp.logical_not(safe))
        def _():
            key_rows, value_rows = attention.rows_of(tile)
            largest_ref[...] = jnp.full((1, TILE), mask_value, jnp.float32)
            total_ref[...] = jnp.zeros((1, TILE), jnp.float32)
            accum_ref[...] = jnp.zeros((HEAD_DIM, TILE), jnp.float32)
            for source, core in ((own, attention.core), (peer, other)):

                def block(index, _, source=source, core=core):
                    mark = attention.key_mark(index, core)
                    key_tile = jnp.concatenate([source[index, key_rows], mark], axis=1)
                    scores = nt(key_tile, queries[tile])
                    largest = largest_ref[...]
                    top = jnp.maximum(largest, jnp.max(scores, axis=0, keepdims=True))
                    rescale = jnp.exp2((largest - top) * to_base2)
                    expo = jnp.exp2((scores - top) * to_base2)
                    largest_ref[...] = top
                    total_ref[...] = total_ref[...] * rescale + jnp.sum(
                        expo, axis=0, keepdims=True
                    )
                    accum_ref[...] = accum_ref[...] * rescale + jnp.dot(
                        source[index, value_rows],
                        expo.astype(jnp.bfloat16),
                        preferred_element_type=jnp.float32,
                    )
                    return 0

                lax.fori_loop(0, CHIPS, block, 0)
            store(tile, accum_ref[...], total_ref[...])

        return 0

    lax.fori_loop(0, TILES, visit, 0)
    main = CHIPS * ROWS // TILE
    out[:, 0:ROWS] = results[0:main].reshape(CHIPS, ROWS, HEAD_DIM)
    out[:, ROWS:Q_ROWS] = results[main:TILES].reshape(CHIPS, HALF, HEAD_DIM)


def restore_kernel(returned, out, sems):
    copies = []
    for chip in range(CHIPS):
        main, shared, row = heads_of(chip)
        for source, target in (
            (returned.at[chip, 0:ROWS], out.at[:, columns(main)]),
            (returned.at[chip, ROWS:Q_ROWS], out.at[row : row + HALF, columns(shared)]),
        ):
            copy = pltpu.make_async_copy(source, target, sems.at[len(copies)])
            copy.start()
            copies.append(copy)
    for copy in copies:
        copy.wait()


def body(
    latents,
    modulation_shift,
    modulation_scale,
    query,
    key,
    value,
    adapter_down_weight,
    adapter_up_weight,
    adapter_index,
    adapter_weight,
    sequence_length,
):
    same_core = [[2 * c + k for c in range(CHIPS)] for k in range(2)]
    vmem = pl.BlockSpec(memory_space=pltpu.VMEM)
    smem = pl.BlockSpec(memory_space=pltpu.SMEM)
    anywhere = pl.BlockSpec(memory_space=pl.ANY)
    params = pltpu.CompilerParams(vmem_limit_bytes=36 * 1024 * 1024)
    width = HEADS * HEAD_DIM
    wide, dma = jnp.bfloat16, pltpu.SemaphoreType.DMA

    send = pl.pallas_call(
        prepare_kernel,
        out_shape=jax.ShapeDtypeStruct((CHIPS, PIECE, HEAD_DIM), wide),
        in_specs=[smem, anywhere, vmem, vmem] + [anywhere] * 5 + [vmem, vmem],
        out_specs=vmem,
        scratch_shapes=[
            pltpu.VMEM((ROWS, width), wide),
            pltpu.VMEM((ROWS, width), wide),
            pltpu.VMEM((ROWS, width), wide),
            pltpu.VMEM((ROWS, width), wide),
            pltpu.VMEM((width, ROWS), wide),
            pltpu.VMEM((ROWS, width), wide),
            dma((6,)),
        ],
        compiler_params=params,
        name="prepare",
    )(
        *(
            pltpu.with_memory_space_constraint(operand, pltpu.HBM)
            for operand in (
                sequence_length,
                latents[0],
                modulation_shift[0],
                modulation_scale[0],
                query[0],
                key[0],
                value[0],
                adapter_down_weight,
                adapter_up_weight,
                adapter_index[0].T,
                adapter_weight[0].T,
            )
        )
    )
    own = lax.all_to_all(
        send, "seq", split_axis=0, concat_axis=0, tiled=True, axis_index_groups=same_core
    )
    peer = lax.ppermute(own, "seq", [(d, d ^ 1) for d in range(2 * CHIPS)])
    pairs = TILES * TILE * PACK_TOKENS // 2
    cost = pl.CostEstimate(
        flops=6 * HEAD_DIM * pairs, bytes_accessed=4 << 20, transcendentals=pairs
    )
    marks = pltpu.VMEM((CHIPS, ROWS, HEAD_DIM), wide)
    weights = pltpu.VMEM((2, STEP * ROWS, TILE), wide)
    state = pl.pallas_call(
        own_kernel,
        out_shape=[
            jax.ShapeDtypeStruct((TILES, HEAD_DIM, TILE), jnp.float32),
            jax.ShapeDtypeStruct((TILES, 8, TILE), jnp.float32),
            jax.ShapeDtypeStruct((TILES, TILE, 2 * HEAD_DIM), wide),
            jax.ShapeDtypeStruct((CHIPS, ROWS, HEAD_DIM), wide),
        ],
        in_specs=[smem, vmem],
        out_specs=[vmem] * 4,
        scratch_shapes=[pltpu.VMEM((ROWS, HEAD_DIM), wide), marks, weights],
        compiler_params=params,
        cost_estimate=cost,
        name="attend_own",
    )(sequence_length, own)
    attended = pl.pallas_call(
        peer_kernel,
        out_shape=jax.ShapeDtypeStruct((CHIPS, Q_ROWS, HEAD_DIM), wide),
        in_specs=[smem] + [vmem] * 6,
        out_specs=vmem,
        scratch_shapes=[
            weights,
            pltpu.VMEM((TILES, TILE, HEAD_DIM), wide),
            pltpu.VMEM((1, TILE), jnp.float32),
            pltpu.VMEM((1, TILE), jnp.float32),
            pltpu.VMEM((HEAD_DIM, TILE), jnp.float32),
        ],
        compiler_params=params,
        cost_estimate=cost,
        name="attend_peer",
    )(sequence_length, own, peer, *state)
    returned = lax.all_to_all(
        attended, "seq", split_axis=0, concat_axis=0, tiled=True, axis_index_groups=same_core
    )
    restored = pl.pallas_call(
        restore_kernel,
        out_shape=jax.ShapeDtypeStruct((ROWS, width), wide),
        in_specs=[vmem],
        out_specs=anywhere,
        scratch_shapes=[dma((2 * CHIPS,))],
        compiler_params=params,
        name="restore",
    )(returned)
    return restored[None]


def solution(mesh):
    in_specs = (
        P("dp", "seq", None),
        P("dp", None, None),
        P("dp", None, None),
        P("dp", "seq", None),
        P("dp", "seq", None),
        P("dp", "seq", None),
        P(),
        P(),
        P("dp", "seq", None),
        P("dp", "seq", None),
        P("dp", None),
    )
    out_specs = P("dp", "seq", None)
    return jax.shard_map(body, mesh=mesh, in_specs=in_specs, out_specs=out_specs, check_vma=False)
```

```python
import functools
import math

import jax
import jax.numpy as jnp
from jax import lax
from jax.experimental import pallas as pl
from jax.experimental.pallas import tpu as pltpu
from jax.sharding import PartitionSpec as P

HEADS = 24
HEAD_DIM = 128
STYLE_ADAPTERS = 8
ADAPTER_RANK = 16
ROWS = 128
CHIPS = 16
PACK_TOKENS = 4096
BLOCKS = PACK_TOKENS // ROWS
HALF = ROWS // 2
Q_ROWS = ROWS + HALF
K_AT = Q_ROWS
V_AT = K_AT + 2 * ROWS
PIECE = V_AT + 2 * ROWS
KV_ROWS = 4 * ROWS
TILE = 1024
TILES = CHIPS * Q_ROWS // TILE
STEP = 16
SAFE_LOW, SAFE_HIGH = 2.0**-60, 2.0**100

mask_value = -1e30
epsilon = 1e-06
to_base2 = math.log2(math.e) / math.sqrt(HEAD_DIM)


def heads_of(chip):
    trio = 3 * (chip // 2)
    if chip % 2 == 0:
        return trio, trio + 1, 0
    return trio + 2, trio + 1, HALF


def columns(head):
    return slice(head * HEAD_DIM, (head + 1) * HEAD_DIM)


def prepare_kernel(
    lengths, latents, shift, scale, query, key, value, down, up, index, weight, send,
    latents_in, query_in, key_in, value_in, down_in, up_in, in_sems,
):
    pairs = (
        (latents, latents_in),
        (down, down_in),
        (up, up_in),
        (value, value_in),
        (query, query_in),
        (key, key_in),
    )
    loads = [
        pltpu.make_async_copy(source, target, in_sems.at[n])
        for n, (source, target) in enumerate(pairs)
    ]
    for load in loads:
        load.start()
    first = lengths[0, 0]
    second = first + lengths[0, 1]
    start = lax.axis_index("seq") * ROWS
    shape = (ROWS, ROWS)
    adapter = lax.broadcasted_iota(jnp.int32, shape, 0) // ADAPTER_RANK
    coefficient = jnp.zeros(shape, jnp.float32)
    for slot in range(index.shape[0]):
        coefficient += jnp.where(
            adapter == index[slot : slot + 1, :], weight[slot : slot + 1, :], 0.0
        )
    coefficient = coefficient.T
    segments = shift.shape[0]
    token = start + lax.broadcasted_iota(jnp.int32, (ROWS, segments), 0)
    segment = (token >= first).astype(jnp.int32) + (token >= second).astype(jnp.int32)
    lane = lax.broadcasted_iota(jnp.int32, (ROWS, segments), 1)
    chosen = jnp.where(lane == segment, 1.0, 0.0).astype(jnp.bfloat16)

    width = latents_in.shape[1]
    wide = 512
    chunks = width // wide

    def lanes_of(chunk):
        return slice(chunk * wide, (chunk + 1) * wide)

    def folded(values):
        parts = [values[:, n * HEAD_DIM : (n + 1) * HEAD_DIM] for n in range(wide // HEAD_DIM)]
        return functools.reduce(jnp.add, parts)

    loads[0].wait()
    zeros = jnp.zeros((ROWS, HEAD_DIM), jnp.float32)
    sums = zeros
    for n in range(chunks):
        sums += folded(latents_in[:, lanes_of(n)].astype(jnp.float32))
    center = jnp.sum(sums, axis=1, keepdims=True) * (1.0 / width)
    sums = zeros
    for n in range(chunks):
        spread = latents_in[:, lanes_of(n)].astype(jnp.float32) - center
        sums += folded(spread * spread)
    variance = jnp.sum(sums, axis=1, keepdims=True) * (1.0 / width)
    inverse = 1.0 / jnp.sqrt(variance + epsilon)
    loads[1].wait()
    low_rank = zeros
    for n in range(chunks):
        lanes = lanes_of(n)
        normed = (latents_in[:, lanes].astype(jnp.float32) - center) * inverse
        scales = jnp.dot(chosen, scale[:, lanes], preferred_element_type=jnp.float32)
        shifts = jnp.dot(chosen, shift[:, lanes], preferred_element_type=jnp.float32)
        modulated = ((1.0 + scales) * normed + shifts).astype(jnp.bfloat16)
        low_rank += jnp.dot(modulated, down_in[lanes, :], preferred_element_type=jnp.float32)
    scaled = (low_rank * coefficient).astype(jnp.bfloat16)
    for load in loads[2:]:
        load.wait()
    trio = 3 * HEAD_DIM

    for pair in range(CHIPS // 2):
        lanes = slice(pair * trio, (pair + 1) * trio)
        update = jnp.dot(scaled, up_in[:, lanes], preferred_element_type=jnp.float32)
        mixed = value_in[:, lanes].astype(jnp.float32) + update
        turned = [mixed[:, columns(head)].T.astype(jnp.bfloat16) for head in range(3)]
        for side in range(2):
            main, shared, row = heads_of(side)
            main_at, shared_at = columns(3 * pair + main), columns(3 * pair + shared)
            chip = 2 * pair + side
            send[chip, 0:ROWS] = query_in[:, main_at]
            send[chip, ROWS:Q_ROWS] = query_in[row : row + HALF, shared_at]
            send[chip, K_AT : K_AT + ROWS] = key_in[:, main_at]
            send[chip, K_AT + ROWS : V_AT] = key_in[:, shared_at]
            send[chip, V_AT : V_AT + ROWS] = turned[main]
            send[chip, V_AT + ROWS : PIECE] = turned[shared]


def nt(left, right):
    return lax.dot_general(
        left, right, (((1,), (1,)), ((), ())), preferred_element_type=jnp.float32
    )


class Attention:
    def __init__(self, lengths):
        self.first = lengths[0, 0]
        self.second = self.first + lengths[0, 1]
        device = lax.axis_index("seq")
        self.core = lax.rem(device, 2)
        self.shared_row = lax.rem(lax.div(device, 2), 2) * HALF

    def same_segment_lane(self, source, core):
        shape = (ROWS, HEAD_DIM)
        token = (2 * source + core) * ROWS + lax.broadcasted_iota(jnp.int32, shape, 0)
        segment = (token >= self.first).astype(jnp.int32)
        segment += (token >= self.second).astype(jnp.int32)
        lane = lax.broadcasted_iota(jnp.int32, shape, 1)
        return lane == segment, lane

    def key_mark(self, source, core):
        same, lane = self.same_segment_lane(source, core)
        return jnp.where(same | (lane >= 3), 0.0, mask_value).astype(jnp.bfloat16)

    def fill(self, own, queries, query_mark, key_marks, peer_marks):
        low, high = slice(0, HEAD_DIM), slice(HEAD_DIM, 2 * HEAD_DIM)
        main, shared = TILE // ROWS, TILE // HALF

        def visit(source, _):
            same, _ = self.same_segment_lane(source, self.core)
            query_mark[...] = jnp.where(same, 1.0, 0.0).astype(jnp.bfloat16)
            key_marks[source] = self.key_mark(source, self.core)
            peer_marks[source] = self.key_mark(source, 1 - self.core)
            tile = lax.div(source, main)
            rows = pl.ds(pl.multiple_of(lax.rem(source, main) * ROWS, ROWS), ROWS)
            queries[tile, rows, low] = own[source, 0:ROWS]
            queries[tile, rows, high] = query_mark[...]
            tile = CHIPS // main + lax.div(source, shared)
            rows = pl.ds(pl.multiple_of(lax.rem(source, shared) * HALF, HALF), HALF)
            queries[tile, rows, low] = own[source, ROWS:Q_ROWS]
            mark_rows = pl.ds(pl.multiple_of(self.shared_row, HALF), HALF)
            queries[tile, rows, high] = query_mark[mark_rows, :]
            return 0

        lax.fori_loop(0, CHIPS, visit, 0)

    def rows_of(self, tile):
        kind = (tile >= CHIPS * ROWS // TILE).astype(jnp.int32)
        key_rows = pl.ds(pl.multiple_of(K_AT + kind * ROWS, HALF), ROWS)
        value_rows = pl.ds(pl.multiple_of(V_AT + kind * ROWS, HALF), ROWS)
        return key_rows, value_rows

    def add(self, tile, queries, source, marks, weights, total, accum):
        key_rows, value_rows = self.rows_of(tile)
        steps, count = CHIPS // STEP, STEP * ROWS
        for step in range(steps + 1):
            if step < steps:
                blocks = slice(step * STEP, (step + 1) * STEP)
                key_tile = source[blocks, key_rows].reshape(count, HEAD_DIM)
                mark = marks[blocks].reshape(count, HEAD_DIM)
                scores = nt(jnp.concatenate([key_tile, mark], axis=1), queries)
                expo = jnp.exp2(scores * to_base2)
                sums = jnp.sum(expo.reshape(count // 8, 8, TILE), axis=0)
                total = sums if total is None else total + sums
                weights[step % 2] = expo.astype(jnp.bfloat16)
            if step > 0:
                start = (step - 1) * STEP
                value_tile = [source[start + n, value_rows] for n in range(STEP)]
                part = jnp.dot(
                    jnp.concatenate(value_tile, axis=1),
                    weights[(step - 1) % 2],
                    preferred_element_type=jnp.float32,
                )
                accum = part if accum is None else accum + part
        return total, accum


def own_kernel(lengths, own, accums, totals, queries, peer_marks, query_mark, key_marks, weights):
    attention = Attention(lengths)
    attention.fill(own, queries, query_mark, key_marks, peer_marks)

    def visit(tile, _):
        total, accum = attention.add(tile, queries[tile], own, key_marks, weights, None, None)
        accums[tile] = accum
        totals[tile] = total
        return 0

    lax.fori_loop(0, TILES, visit, 0)


def peer_kernel(
    lengths, own, peer, accums, totals, queries, key_marks, out, weights,
    results, largest_ref, total_ref, accum_ref,
):
    attention = Attention(lengths)
    other = 1 - attention.core

    def store(tile, accum, total):
        results[tile] = (accum * (1.0 / total)).T.astype(jnp.bfloat16)

    def visit(tile, _):
        total, accum = attention.add(
            tile, queries[tile], peer, key_marks, weights, totals[tile], accums[tile]
        )
        total = jnp.sum(total, axis=0, keepdims=True)
        store(tile, accum, total)

        safe = (jnp.max(total) < SAFE_HIGH) & (jnp.min(total) > SAFE_LOW)

        @pl.when(jnp.logical_not(safe))
        def _():
            key_rows, value_rows = attention.rows_of(tile)
            largest_ref[...] = jnp.full((1, TILE), mask_value, jnp.float32)
            total_ref[...] = jnp.zeros((1, TILE), jnp.float32)
            accum_ref[...] = jnp.zeros((HEAD_DIM, TILE), jnp.float32)
            for source, core in ((own, attention.core), (peer, other)):

                def block(index, _, source=source, core=core):
                    mark = attention.key_mark(index, core)
                    key_tile = jnp.concatenate([source[index, key_rows], mark], axis=1)
                    scores = nt(key_tile, queries[tile])
                    largest = largest_ref[...]
                    top = jnp.maximum(largest, jnp.max(scores, axis=0, keepdims=True))
                    rescale = jnp.exp2((largest - top) * to_base2)
                    expo = jnp.exp2((scores - top) * to_base2)
                    largest_ref[...] = top
                    total_ref[...] = total_ref[...] * rescale + jnp.sum(
                        expo, axis=0, keepdims=True
                    )
                    accum_ref[...] = accum_ref[...] * rescale + jnp.dot(
                        source[index, value_rows],
                        expo.astype(jnp.bfloat16),
                        preferred_element_type=jnp.float32,
                    )
                    return 0

                lax.fori_loop(0, CHIPS, block, 0)
            store(tile, accum_ref[...], total_ref[...])

        return 0

    lax.fori_loop(0, TILES, visit, 0)
    main = CHIPS * ROWS // TILE
    out[:, 0:ROWS] = results[0:main].reshape(CHIPS, ROWS, HEAD_DIM)
    out[:, ROWS:Q_ROWS] = results[main:TILES].reshape(CHIPS, HALF, HEAD_DIM)


def restore_kernel(returned, out, sems):
    copies = []
    for chip in range(CHIPS):
        main, shared, row = heads_of(chip)
        for source, target in (
            (returned.at[chip, 0:ROWS], out.at[:, columns(main)]),
            (returned.at[chip, ROWS:Q_ROWS], out.at[row : row + HALF, columns(shared)]),
        ):
            copy = pltpu.make_async_copy(source, target, sems.at[len(copies)])
            copy.start()
            copies.append(copy)
    for copy in copies:
        copy.wait()


def body(
    latents,
    modulation_shift,
    modulation_scale,
    query,
    key,
    value,
    adapter_down_weight,
    adapter_up_weight,
    adapter_index,
    adapter_weight,
    sequence_length,
):
    same_core = [[2 * c + k for c in range(CHIPS)] for k in range(2)]
    vmem = pl.BlockSpec(memory_space=pltpu.VMEM)
    smem = pl.BlockSpec(memory_space=pltpu.SMEM)
    anywhere = pl.BlockSpec(memory_space=pl.ANY)
    params = pltpu.CompilerParams(vmem_limit_bytes=36 * 1024 * 1024)
    width = HEADS * HEAD_DIM
    wide, dma = jnp.bfloat16, pltpu.SemaphoreType.DMA

    send = pl.pallas_call(
        prepare_kernel,
        out_shape=jax.ShapeDtypeStruct((CHIPS, PIECE, HEAD_DIM), wide),
        in_specs=[smem, anywhere, vmem, vmem] + [anywhere] * 5 + [vmem, vmem],
        out_specs=vmem,
        scratch_shapes=[
            pltpu.VMEM((ROWS, width), wide),
            pltpu.VMEM((ROWS, width), wide),
            pltpu.VMEM((ROWS, width), wide),
            pltpu.VMEM((ROWS, width), wide),
            pltpu.VMEM((width, ROWS), wide),
            pltpu.VMEM((ROWS, width), wide),
            dma((6,)),
        ],
        compiler_params=params,
        name="prepare",
    )(
        *(
            pltpu.with_memory_space_constraint(operand, pltpu.HBM)
            for operand in (
                sequence_length,
                latents[0],
                modulation_shift[0],
                modulation_scale[0],
                query[0],
                key[0],
                value[0],
                adapter_down_weight,
                adapter_up_weight,
                adapter_index[0].T,
                adapter_weight[0].T,
            )
        )
    )
    own = lax.all_to_all(
        send, "seq", split_axis=0, concat_axis=0, tiled=True, axis_index_groups=same_core
    )
    peer = lax.ppermute(own, "seq", [(d, d ^ 1) for d in range(2 * CHIPS)])
    pairs = TILES * TILE * PACK_TOKENS // 2
    cost = pl.CostEstimate(
        flops=6 * HEAD_DIM * pairs, bytes_accessed=4 << 20, transcendentals=pairs
    )
    marks = pltpu.VMEM((CHIPS, ROWS, HEAD_DIM), wide)
    weights = pltpu.VMEM((2, STEP * ROWS, TILE), wide)
    state = pl.pallas_call(
        own_kernel,
        out_shape=[
            jax.ShapeDtypeStruct((TILES, HEAD_DIM, TILE), jnp.float32),
            jax.ShapeDtypeStruct((TILES, 8, TILE), jnp.float32),
            jax.ShapeDtypeStruct((TILES, TILE, 2 * HEAD_DIM), wide),
            jax.ShapeDtypeStruct((CHIPS, ROWS, HEAD_DIM), wide),
        ],
        in_specs=[smem, vmem],
        out_specs=[vmem] * 4,
        scratch_shapes=[pltpu.VMEM((ROWS, HEAD_DIM), wide), marks, weights],
        compiler_params=params,
        cost_estimate=cost,
        name="attend_own",
    )(sequence_length, own)
    attended = pl.pallas_call(
        peer_kernel,
        out_shape=jax.ShapeDtypeStruct((CHIPS, Q_ROWS, HEAD_DIM), wide),
        in_specs=[smem] + [vmem] * 6,
        out_specs=vmem,
        scratch_shapes=[
            weights,
            pltpu.VMEM((TILES, TILE, HEAD_DIM), wide),
            pltpu.VMEM((1, TILE), jnp.float32),
            pltpu.VMEM((1, TILE), jnp.float32),
            pltpu.VMEM((HEAD_DIM, TILE), jnp.float32),
        ],
        compiler_params=params,
        cost_estimate=cost,
        name="attend_peer",
    )(sequence_length, own, peer, *state)
    returned = lax.all_to_all(
        attended, "seq", split_axis=0, concat_axis=0, tiled=True, axis_index_groups=same_core
    )
    restored = pl.pallas_call(
        restore_kernel,
        out_shape=jax.ShapeDtypeStruct((ROWS, width), wide),
        in_specs=[vmem],
        out_specs=anywhere,
        scratch_shapes=[dma((2 * CHIPS,))],
        compiler_params=params,
        name="restore",
    )(returned)
    return restored[None]


def solution(mesh):
    in_specs = (
        P("dp", "seq", None),
        P("dp", None, None),
        P("dp", None, None),
        P("dp", "seq", None),
        P("dp", "seq", None),
        P("dp", "seq", None),
        P(),
        P(),
        P("dp", "seq", None),
        P("dp", "seq", None),
        P("dp", None),
    )
    out_specs = P("dp", "seq", None)
    return jax.shard_map(body, mesh=mesh, in_specs=in_specs, out_specs=out_specs, check_vma=False)
```
